1024 devices in a mesh: node: 128 (over z_lo, y, core), local: 8 (over z_hi, x).
Axes of the slice: x: 4, y: 8, z: 16 (z_hi: 2, z_lo: 8; z = z_hi * 8 + z_lo), core: 2. Of those that a mesh axis runs over, the one named last changes fastest.
Arguments:
- tokens: bfloat16 [131072, 4096], P('node'), may hold values from -6 to 6
- hidden_grad: bfloat16 [131072, 768], P('node', 'local'), may hold values from -6 to 6
- master: float32 [2, 4096, 768], P(None, 'node', 'local'), may hold values from -0.09375 to 0.09375
- counts: int32 [1024], P(('node', 'local')), may hold values from 0 to 128, as said below
Outputs:
- hidden: bfloat16 [131072, 768], P('node', 'local')
- weight_grad: float32 [2, 4096, 768], P(None, 'node', 'local')
The draws below stay inside these ranges and needn't reach their ends.
Inputs may be any that keep to these rules, and one draw needn't show every extreme that they name: `counts`: each count is a multiple of 16; some device is full in every draw.
All inputs are finite; a program needn't handle non-finite values.
Results may differ from the reference program's by a relative error of at most 0.0058.
Values may be sent and summed in bfloat16 or wider, within the bound.
A program may use at most 32 MiB of HBM per device.

```python
import jax
import jax.numpy as jnp

D = 4096
FF = 768
ROWS_DEV = 128
BLOCK = 16
TOKENS = 131072
N_NODE = 128
N_LOCAL = 8


def draw_counts(key, part):
    key = jax.random.fold_in(key, 5)
    first, second = jax.random.split(key)
    total_dev = N_NODE * N_LOCAL
    per_dev = ROWS_DEV // BLOCK
    blocks = jax.random.randint(first, (total_dev,), 0, per_dev + 1)
    chosen = jax.random.randint(second, (), 0, total_dev)
    blocks = jnp.where(jnp.arange(total_dev) == chosen, per_dev, blocks)
    return (blocks * BLOCK).astype(jnp.int32)


def level_of(rng, dims, cuts, smallest, top_value):
    level, own = 1.0, jax.random.fold_in(rng, 6)
    for dim, blocks in cuts:
        heights = jnp.exp(jax.random.uniform(jax.random.fold_in(own, dim), (blocks,), jnp.float32, smallest / len(cuts), top_value / len(cuts)))
        level = level * jnp.repeat(heights, dims[dim] // blocks).reshape([-1 if axis == dim else 1 for axis in range(len(dims))])
    return level


def bell_draw(stream_key, extent, deviation, reach, cuts=(), held_as=jnp.bfloat16):
    array = deviation * jax.random.normal(stream_key, extent, jnp.float32)
    if cuts:
        array = array * level_of(stream_key, extent, cuts, -0.22, 0.18)
    return jnp.clip(array, -reach, reach).astype(held_as)


def setup_inputs(seed: int = 0) -> dict:
    streams_of = jax.random.split(jax.random.key(seed), 5)
    tokens = bell_draw(streams_of[0], (TOKENS, D), 1.0, 6.0, ((0, 128),))
    hidden_grad = bell_draw(streams_of[1], (TOKENS, FF), 1.0, 6.0, ((0, 128), (1, 8)))
    master = bell_draw(streams_of[2], (2, D, FF), D ** -0.5, 0.09375, ((1, 128), (2, 8)), jnp.float32)
    counts = draw_counts(jax.random.fold_in(streams_of[4], 71), 0)
    return {"tokens": tokens, "hidden_grad": hidden_grad, "master": master, "counts": counts}


def reference(tokens, hidden_grad, master, counts):
    weights = master.astype(jnp.bfloat16)
    w_gate = weights[0]
    w_up = weights[1]
    position = jnp.arange(TOKENS, dtype=jnp.int32)
    limits = jnp.broadcast_to(counts[:, None], (counts.shape[0], ROWS_DEV)).reshape(-1)
    live = (position % ROWS_DEV < limits).astype(jnp.float32)[:, None]
    gate = jnp.dot(tokens, w_gate, preferred_element_type=jnp.float32)
    up = jnp.dot(tokens, w_up, preferred_element_type=jnp.float32)
    sigmoid_gate = jax.nn.sigmoid(gate)
    activated = gate * sigmoid_gate
    hidden = (live * activated * up).astype(jnp.bfloat16)
    upstream = live * hidden_grad.astype(jnp.float32)
    gate_cot = (upstream * up * sigmoid_gate * (1.0 + gate * (1.0 - sigmoid_gate))).astype(jnp.bfloat16)
    up_cot = (upstream * activated).astype(jnp.bfloat16)
    scale = 1.0 / jnp.sqrt(jnp.float32(TOKENS))
    grad_gate = jnp.dot(tokens.T, gate_cot, preferred_element_type=jnp.float32) * scale
    grad_up = jnp.dot(tokens.T, up_cot, preferred_element_type=jnp.float32) * scale
    return (hidden, jnp.stack([grad_gate, grad_up]))
```

```python
import jax
import jax.numpy as jnp
from jax import lax
from jax.experimental import pallas as pl
from jax.experimental.pallas import tpu as pltpu
from jax.sharding import PartitionSpec as P

BF16 = jnp.bfloat16
F32 = jnp.float32
MESH = pl.DeviceIdType.MESH

NZ, NY = 8, 8
ROWS, WIDTH = 32, 96
PACKED = 48


def pack(block):
    tail = jnp.concatenate([block[..., :16, 128:192], block[..., 16:32, 128:192]], axis=-1)
    return jnp.concatenate([block[..., :128], tail], axis=-2)


def kernel(
    tok_hbm, hg_hbm, master_ref, counts_ref,
    hid_hbm, wg_ref,
    tok, tokT, hg, hgT, wbuf, w_y, acc, cotT, hidT, hid, cnt,
    part, xsend, xrecv, rsend, rrecv, own, zsend, zrecv,
    tok_sem, hg_sem, hid_sem,
    cnt_s, cnt_r, az_s, az_r, ay_s, ay_r, ac_s, ac_r,
    rc_s, rc_r, ry_s, ry_r, rz_s, rz_r,
):
    node, loc = lax.axis_index("node"), lax.axis_index("local")
    z, y, c = node // (2 * NY), (node // 2) % NY, node % 2
    rows = tok.shape[1]
    chunk = tok.shape[2]

    def at(z_, y_, c_):
        return ((z_ * NY + y_) * 2 + c_, loc)

    def ring(offset):
        return lax.rem(y + offset + 2 * NY, NY)

    right, left, twin = at(z, ring(1), c), at(z, ring(-1), c), at(z, y, 1 - c)
    z_peers = [at(lax.rem(z + i, NZ), y, c) for i in range(1, NZ)]
    l_peers = [(node, lax.rem(loc + i, 8)) for i in range(1, 8)]

    tok_copies = [
        pltpu.make_async_copy(tok_hbm.at[:, pl.ds(i * chunk, chunk)], tok.at[i], tok_sem.at[i])
        for i in range(NZ)
    ]
    hg_copy = pltpu.make_async_copy(hg_hbm, hg, hg_sem)
    barrier = pltpu.get_barrier_semaphore()
    peers = [right, left, twin] + z_peers + l_peers
    for peer in peers:
        pl.semaphore_signal(barrier, inc=1, device_id=peer, device_id_type=MESH)
    for copy in tok_copies:
        copy.start()
    hg_copy.start()
    both = jnp.concatenate([master_ref[0], master_ref[1]], axis=1)
    wbuf[c, y, z] = pack(both).astype(BF16)
    cnt[loc] = jnp.full((8, 128), counts_ref[0], jnp.int32)
    pl.semaphore_wait(barrier, len(peers))

    sends = []

    def remote(src, dst, s_sem, r_sem, device):
        return pltpu.make_async_remote_copy(
            src_ref=src, dst_ref=dst, send_sem=s_sem, recv_sem=r_sem,
            device_id=device, device_id_type=MESH,
        )

    def push(copy):
        copy.start()
        sends.append(copy)

    for i in range(1, NZ):
        push(remote(wbuf.at[c, y, z], wbuf.at[c, y, z], az_s.at[i], az_r.at[z], z_peers[i - 1]))
    for i in range(1, 8):
        push(remote(cnt.at[loc], cnt.at[loc], cnt_s.at[i], cnt_r.at[loc], l_peers[i - 1]))

    near = z // 4

    def half(k):
        return near if k == 0 else 1 - near

    def transpose(i):
        tok_copies[i].wait()
        tokT[i] = tok[i].T.reshape(NY, chunk // NY, rows)

    def ay(d, s, k):
        origin = ring(1 - s) if d == 0 else ring(s - 1)
        block = wbuf.at[c, origin, pl.ds(4 * half(k), 4)]
        return remote(block, block, ay_s.at[d, s - 1, k], ay_r.at[d, s - 1, k], right if d == 0 else left)

    def ac(offset, k, to=None):
        block = wbuf.at[c if to is None else 1 - c, ring(offset), pl.ds(4 * half(k), 4)]
        return remote(block, block, ac_s.at[offset % NY, k], ac_r.at[offset % NY, k], twin)

    def forward(offset):
        for k in range(2):
            ac(offset, k, to=0).wait_recv()
        o = ring(offset)
        for core in range(2):
            for j in range(NZ):
                r = j * 64 + core * ROWS
                got = wbuf[core, o, j]
                w_y[r : r + ROWS, :128] = got[:ROWS]
                w_y[r : r + 16, 128:192] = got[ROWS:, :64]
                w_y[r + 16 : r + 32, 128:192] = got[ROWS:, 64:]
        x = tokT[:, o].reshape(chunk, rows)
        d = lax.dot_general(w_y[...], x, (((0,), (0,)), ((), ())), preferred_element_type=F32)
        if offset == 0:
            acc[...] = d
        else:
            acc[...] += d

    for i in range(4):
        transpose(i)
    for k in range(2):
        for j in range(4):
            origin = 4 * half(k) + j

            @pl.when(origin != z)
            def _():
                block = wbuf.at[c, y, origin]
                remote(block, block, az_s.at[0], az_r.at[origin], twin).wait_recv()

        for d in range(2):
            push(ay(d, 1, k))
        push(ac(0, k))
        if k == 0:
            for i in range(4, 8):
                transpose(i)
    hg_copy.wait()
    hgT[...] = hg[...].T
    for s in range(2, 6):
        for k in range(2):
            for d in range(2):
                if s - 1 == 4 and d != k:
                    continue
                ay(d, s - 1, k).wait_recv()
                if s <= 3 or (s == 4 and d == k):
                    push(ay(d, s, k))
                push(ac(1 - s if d == 0 else s - 1, k) if s < 5 else ac(4, k))
        if s == 2:
            forward(0)
        elif s > 2:
            forward(s - 2)
            forward(2 - s)
    for i in range(1, 8):
        slot = cnt.at[lax.rem(loc + i, 8)]
        remote(slot, slot, cnt_s.at[0], cnt_r.at[lax.rem(loc + i, 8)], twin).wait_recv()
    forward(4)

    for j in range(8):
        lanes = slice(j * 128, (j + 1) * 128)
        live = (lax.broadcasted_iota(jnp.int32, (8, 128), 1) < cnt[j]).astype(F32)[:1]
        gate, up = acc[:WIDTH, lanes], acc[WIDTH:, lanes]
        sig = jax.nn.sigmoid(gate)
        activated = gate * sig
        hidT[:, lanes] = (live * activated * up).astype(BF16)
        upstream = live * hgT[:, lanes].astype(F32)
        cotT[:WIDTH, lanes] = (upstream * up * sig * (1.0 + gate * (1.0 - sig))).astype(BF16)
        cotT[WIDTH:, lanes] = (upstream * activated).astype(BF16)

    def rc(offset):
        i = offset % NY
        return remote(xsend.at[i], xrecv.at[i], rc_s.at[i], rc_r.at[i], twin)

    def backward(offset):
        i = offset % NY
        x = tokT[:, ring(offset)].reshape(chunk, rows)
        g = lax.dot_general(x, cotT[...], (((1,), (1,)), ((), ())), preferred_element_type=F32)
        part[i] = g.reshape(NZ, 2, ROWS, 2 * WIDTH)
        xsend[i] = pack(part[i, :, 1 - c]).astype(BF16)
        push(rc(offset))

    def chip_sum(offset):
        i = offset % NY
        rc(offset).wait_recv()
        own[i] = pack(part[i, :, c]) + xrecv[i].astype(F32)

    def ry(d, s, k):
        h = pl.ds(4 * half(k), 4)
        return remote(
            rsend.at[d, s - 1, h], rrecv.at[d, s - 1, h],
            ry_s.at[d, s - 1, k], ry_r.at[d, s - 1, k], right if d == 0 else left,
        )

    def ry_send(s):
        for k in range(2):
            for d in range(2):
                if s == 1 and d != k:
                    continue
                h = pl.ds(4 * half(k), 4)
                mine = own[(5 - s if d == 0 else s - 5) % NY, h]
                if s > 2 or (s == 2 and d == k):
                    ry(d, s - 1, k).wait_recv()
                    mine = mine + rrecv[d, s - 2, h].astype(F32)
                rsend[d, s - 1, h] = mine.astype(BF16)
                push(ry(d, s, k))

    backward(4)
    backward(3)
    chip_sum(4)
    ry_send(1)
    backward(-3)
    chip_sum(3)
    backward(2)
    chip_sum(-3)
    ry_send(2)
    backward(-2)
    chip_sum(2)
    backward(1)
    chip_sum(-2)
    ry_send(3)
    backward(-1)
    chip_sum(1)
    backward(0)
    chip_sum(-1)
    ry_send(4)
    chip_sum(0)
    hid[...] = hidT[...].T
    hid_copy = pltpu.make_async_copy(hid, hid_hbm, hid_sem)
    hid_copy.start()
    total = own[0]
    for d in range(2):
        for k in range(2):
            ry(d, 4, k).wait_recv()
        total = total + rrecv[d, 3].astype(F32)
    own[0] = total
    zsend[...] = total.astype(BF16)
    for i in range(1, NZ):
        to = lax.rem(z + i, NZ)
        push(remote(zsend.at[to], zrecv.at[i], rz_s.at[i], rz_r.at[i], z_peers[i - 1]))
    grad = own[0, z]
    for i in range(1, NZ):
        remote(zsend.at[0], zrecv.at[i], rz_s.at[i], rz_r.at[i], twin).wait_recv()
        grad = grad + zrecv[i].astype(F32)
    grad = grad * (1.0 / (rows * NZ * NY * 2) ** 0.5)
    tail = jnp.concatenate([grad[ROWS:, :64], grad[ROWS:, 64:]], axis=0)
    wg_ref[0] = grad[:ROWS, :WIDTH]
    wg_ref[1] = jnp.concatenate([grad[:ROWS, WIDTH:], tail], axis=1)
    for copy in sends:
        copy.wait_send()
    hid_copy.wait()


def on_device(tokens, hidden_grad, master, counts):
    rows, depth = tokens.shape
    chunk = depth // NZ
    dma = pltpu.SemaphoreType.DMA
    vmem = pltpu.VMEM
    return pl.pallas_call(
        kernel,
        out_shape=(
            jax.ShapeDtypeStruct(hidden_grad.shape, BF16),
            jax.ShapeDtypeStruct(master.shape, F32),
        ),
        in_specs=[
            pl.BlockSpec(memory_space=pl.ANY),
            pl.BlockSpec(memory_space=pl.ANY),
            pl.BlockSpec(memory_space=vmem),
            pl.BlockSpec(memory_space=pltpu.SMEM),
        ],
        out_specs=(pl.BlockSpec(memory_space=pl.ANY), pl.BlockSpec(memory_space=vmem)),
        scratch_shapes=[
            vmem((NZ, rows, chunk), BF16),
            vmem((NZ, NY, chunk // NY, rows), BF16),
            vmem((rows, WIDTH), BF16),
            vmem((WIDTH, rows), BF16),
            vmem((2, NY, NZ, PACKED, 128), BF16),
            vmem((chunk, 2 * WIDTH), BF16),
            vmem((2 * WIDTH, rows), F32),
            vmem((2 * WIDTH, rows), BF16),
            vmem((WIDTH, rows), BF16),
            vmem((rows, WIDTH), BF16),
            vmem((8, 8, 128), jnp.int32),
            vmem((NY, NZ, 2, ROWS, 2 * WIDTH), F32),
            vmem((NY, NZ, PACKED, 128), BF16),
            vmem((NY, NZ, PACKED, 128), BF16),
            vmem((2, 4, NZ, PACKED, 128), BF16),
            vmem((2, 4, NZ, PACKED, 128), BF16),
            vmem((NY, NZ, PACKED, 128), F32),
            vmem((NZ, PACKED, 128), BF16),
            vmem((NZ, PACKED, 128), BF16),
            dma((NZ,)), dma, dma,
            dma((8,)), dma((8,)), dma((NZ,)), dma((NZ,)),
            dma((2, 4, 2)), dma((2, 4, 2)), dma((NY, 2)), dma((NY, 2)),
            dma((NY,)), dma((NY,)), dma((2, 4, 2)), dma((2, 4, 2)), dma((NZ,)), dma((NZ,)),
        ],
        compiler_params=pltpu.CompilerParams(
            collective_id=1, has_side_effects=True, vmem_limit_bytes=56 * 2**20
        ),
    )(tokens, hidden_grad, master, counts)


def solution(mesh):
    return jax.shard_map(
        on_device,
        mesh=mesh,
        in_specs=(
            P("node", None),
            P("node", "local"),
            P(None, "node", "local"),
            P(("node", "local")),
        ),
        out_specs=(P("node", "local"), P(None, "node", "local")),
        check_vma=False,
    )
```

```python
import jax
import jax.numpy as jnp
from jax import lax
from jax.experimental import pallas as pl
from jax.experimental.pallas import tpu as pltpu
from jax.sharding import PartitionSpec as P

BF16 = jnp.bfloat16
F32 = jnp.float32
MESH = pl.DeviceIdType.MESH

NZ, NY = 8, 8
ROWS, WIDTH = 32, 96
PACKED = 48


def pack(block):
    tail = jnp.concatenate([block[..., :16, 128:192], block[..., 16:32, 128:192]], axis=-1)
    return jnp.concatenate([block[..., :128], tail], axis=-2)


def kernel(
    tok_hbm, hgT_hbm, master_ref, counts_ref,
    hidT_hbm, wg_ref,
    tok, tokT, hgT, wbuf, w_y, acc, cotT, hidT, cnt,
    part, xsend, xrecv, rsend, rrecv, own, zsend, zrecv,
    tok_sem, hg_sem, hid_sem,
    cx_s, cx_r, ch_s, ch_r, az_u, az_d, az_r, ay_s, ay_r, ac_s, ac_r,
    rc_s, rc_r, ry_s, ry_r, rz_s, rz_r,
):
    node, loc = lax.axis_index("node"), lax.axis_index("local")
    z, y, c = node // (2 * NY), (node // 2) % NY, node % 2
    zh, x = loc // 4, loc % 4
    rows = tok.shape[1]
    chunk = tok.shape[2]

    def at(z_, y_, c_):
        return ((z_ * NY + y_) * 2 + c_, loc)

    def ring(offset):
        return lax.rem(y + offset + 2 * NY, NY)

    right, left, twin = at(z, ring(1), c), at(z, ring(-1), c), at(z, y, 1 - c)
    x_peers = [(node, zh * 4 + lax.rem(x + i, 4)) for i in range(1, 4)]
    partner = (node, (1 - zh) * 4 + x)

    tok_copies = [
        pltpu.make_async_copy(tok_hbm.at[:, pl.ds(i * chunk, chunk)], tok.at[i], tok_sem.at[i])
        for i in range(NZ)
    ]
    hg_copy = pltpu.make_async_copy(hgT_hbm, hgT, hg_sem)
    hid_copy = pltpu.make_async_copy(hidT, hidT_hbm, hid_sem)

    barrier = pltpu.get_barrier_semaphore()

    def greet(peer):
        pl.semaphore_signal(barrier, inc=1, device_id=peer, device_id_type=MESH)

    for i in range(1, NZ):

        @pl.when(z + i < NZ)
        def _():
            greet(at(z + i, y, c))

    @pl.when(z > 0)
    def _():
        greet(at(z - 1, y, c))

    @pl.when(zh == 0)
    def _():
        greet(partner)

    for peer in [right, left, twin] + x_peers:
        greet(peer)
    for copy in tok_copies:
        copy.start()
    hg_copy.start()
    both = jnp.concatenate([master_ref[0], master_ref[1]], axis=1)
    wbuf[c, y, z] = pack(both).astype(BF16)
    cnt[loc] = jnp.full((8, 128), counts_ref[0], jnp.int32)
    pl.semaphore_wait(barrier, 6 + z + zh + jnp.where(z < NZ - 1, 1, 0))

    sends = []

    def remote(src, dst, s_sem, r_sem, device):
        return pltpu.make_async_remote_copy(
            src_ref=src, dst_ref=dst, send_sem=s_sem, recv_sem=r_sem,
            device_id=device, device_id_type=MESH,
        )

    def push(copy):
        copy.start()
        sends.append(copy)

    def transpose(i):
        tok_copies[i].wait()
        tokT[i] = tok[i].T.reshape(NY, chunk // NY, rows)

    pz, ph = z // 2, z // 4
    pairs = [pz, ph * 4 + 1 - pz, 2 - ph, 3 - 3 * ph]

    def pair(k):
        return pl.ds(2 * pairs[k], 2)

    def az_down(i):
        block = wbuf.at[c, y, z]
        return remote(block, block, az_d.at[i], az_r.at[z], at(z - i, y, c))

    def az_up(i):
        block = wbuf.at[c, y, z - i]
        return remote(block, block, az_u.at[i], az_r.at[z - i], at(z + 1, y, c))

    def az_wait(origin):
        block = wbuf.at[c, y, origin]
        remote(block, block, az_u.at[0], az_r.at[origin], twin).wait_recv()

    def relay(i):
        @pl.when(z >= i)
        def _():
            az_wait(z - i)

            @pl.when(z < NZ - 1)
            def _():
                az_up(i).start()

    @pl.when(z < NZ - 1)
    def _():
        az_up(0).start()

    for i in range(NZ - 1, 0, -1):

        @pl.when(z >= i)
        def _():
            az_down(i).start()

    for i in range(3):
        push(remote(cnt.at[loc], cnt.at[loc], cx_s.at[i], cx_r.at[2 - i], x_peers[i]))

    def ay(d, s, k):
        origin = ring(1 - s) if d == 0 else ring(s - 1)
        block = wbuf.at[c, origin, pair(k)]
        return remote(block, block, ay_s.at[d, s - 1, k], ay_r.at[d, s - 1, k], right if d == 0 else left)

    def ac(offset, k, core):
        block = wbuf.at[core, ring(offset), pair(k)]
        return remote(block, block, ac_s.at[offset % NY, k], ac_r.at[offset % NY, k], twin)

    def forward(offset):
        for k in range(4):
            ac(offset, k, 1 - c).wait_recv()
        o = ring(offset)
        for core in range(2):
            for j in range(NZ):
                r = j * 64 + core * ROWS
                got = wbuf[core, o, j]
                w_y[r : r + ROWS, :128] = got[:ROWS]
                w_y[r : r + 16, 128:192] = got[ROWS:, :64]
                w_y[r + 16 : r + 32, 128:192] = got[ROWS:, 64:]
        v = tokT[:, o].reshape(chunk, rows)
        d = lax.dot_general(w_y[...], v, (((0,), (0,)), ((), ())), preferred_element_type=F32)
        if offset == 0:
            acc[...] = d
        else:
            acc[...] += d

    def gather(k, s):
        if s == 0:
            for i in range(2):
                origin = 2 * pairs[k] + i

                @pl.when(origin > z)
                def _():
                    az_wait(origin)

            for d in range(2):
                push(ay(d, 1, k))
            push(ac(0, k, c))
            return
        for d in range(2):
            if s == 4 and d != k % 2:
                continue
            ay(d, s, k).wait_recv()
            if s < 3 or (s == 3 and d == k % 2):
                push(ay(d, s + 1, k))
            push(ac(4 if s == 4 else (-s if d == 0 else s), k, c))

    own_row = cnt.at[pl.ds(zh * 4, 4)]
    other_row = cnt.at[pl.ds((1 - zh) * 4, 4)]
    row_out = remote(own_row, own_row, ch_s, ch_r, partner)
    row_in = remote(other_row, other_row, ch_s, ch_r, partner)

    for t in range(8):
        if t < 4:
            transpose(2 * t)
            transpose(2 * t + 1)
            for i in range(2 * t, 2 * t + 2):
                if i > 0:
                    relay(i)
        elif t == 4:
            forward(0)
        else:
            forward(t - 4)
            forward(4 - t)
        for k in range(4):
            if 0 <= t - k <= 4:
                gather(k, t - k)
        if t == 1:
            for i in range(3):
                slot = cnt.at[zh * 4 + lax.rem(x + 3 - i, 4)]
                remote(slot, slot, cx_s.at[i], cx_r.at[2 - i], twin).wait_recv()

            @pl.when(zh == 1)
            def _():
                row_out.start()

    row_in.wait_recv()

    @pl.when(zh == 0)
    def _():
        row_out.start()

    forward(4)

    for j in range(8):
        lanes = slice(j * 128, (j + 1) * 128)
        live = (lax.broadcasted_iota(jnp.int32, (8, 128), 1) < cnt[j]).astype(F32)[:1]
        gate, up = acc[:WIDTH, lanes], acc[WIDTH:, lanes]
        if j == 0:
            hg_copy.wait()
        sig = jax.nn.sigmoid(gate)
        activated = gate * sig
        hidT[:, lanes] = (live * activated * up).astype(BF16)
        upstream = live * hgT[:, lanes].astype(F32)
        cotT[:WIDTH, lanes] = (upstream * up * sig * (1.0 + gate * (1.0 - sig))).astype(BF16)
        cotT[WIDTH:, lanes] = (upstream * activated).astype(BF16)
    hid_copy.start()

    def rc(offset):
        i = offset % NY
        return remote(xsend.at[i], xrecv.at[i], rc_s.at[i], rc_r.at[i], twin)

    def backward(offset):
        i = offset % NY
        v = tokT[:, ring(offset)].reshape(chunk, rows)
        g = lax.dot_general(v, cotT[...], (((1,), (1,)), ((), ())), preferred_element_type=F32)
        part[i] = g.reshape(NZ, 2, ROWS, 2 * WIDTH)
        xsend[i] = pack(part[i, :, 1 - c]).astype(BF16)
        push(rc(offset))

    def chip_sum(offset):
        i = offset % NY
        rc(offset).wait_recv()
        own[i] = pack(part[i, :, c]) + xrecv[i].astype(F32)

    def ry(d, s, k):
        return remote(
            rsend.at[d, s - 1, pair(k)], rrecv.at[d, s - 1, pair(k)],
            ry_s.at[d, s - 1, k], ry_r.at[d, s - 1, k], right if d == 0 else left,
        )

    def ry_send(s):
        for k in range(3, -1, -1):
            for d in range(2):
                if s == 1 and d != k % 2:
                    continue
                mine = own[(5 - s if d == 0 else s - 5) % NY, pair(k)]
                if s > 2 or (s == 2 and d == k % 2):
                    ry(d, s - 1, k).wait_recv()
                    mine = mine + rrecv[d, s - 2, pair(k)].astype(F32)
                rsend[d, s - 1, pair(k)] = mine.astype(BF16)
                push(ry(d, s, k))

    backward(4)
    backward(3)
    chip_sum(4)
    ry_send(1)
    backward(-3)
    chip_sum(3)
    backward(2)
    chip_sum(-3)
    ry_send(2)
    backward(-2)
    chip_sum(2)
    backward(1)
    chip_sum(-2)
    ry_send(3)
    backward(-1)
    chip_sum(1)
    backward(0)
    chip_sum(-1)
    ry_send(4)
    chip_sum(0)
    zrecv[z] = jnp.zeros(zrecv.shape[1:], BF16)

    def rz(to):
        return remote(zsend.at[to], zrecv.at[z], rz_s.at[to], rz_r.at[z], at(to, y, c))

    for k in range(3, -1, -1):
        total = own[0, pair(k)]
        for d in range(2):
            ry(d, 4, k).wait_recv()
            total = total + rrecv[d, 3, pair(k)].astype(F32)
        own[0, pair(k)] = total
        zsend[pair(k)] = total.astype(BF16)
        for i in range(2):
            to = 2 * pairs[k] + i

            @pl.when(to != z)
            def _():
                rz(to).start()

    for j in range(NZ):

        @pl.when(z != j)
        def _():
            remote(zsend.at[j], zrecv.at[j], rz_s.at[j], rz_r.at[j], twin).wait_recv()

    grad = own[0, z]
    for j in range(NZ):
        grad = grad + zrecv[j].astype(F32)
    grad = grad * (1.0 / (rows * NZ * NY * 2) ** 0.5)
    tail = jnp.concatenate([grad[ROWS:, :64], grad[ROWS:, 64:]], axis=0)
    wg_ref[0] = grad[:ROWS, :WIDTH]
    wg_ref[1] = jnp.concatenate([grad[:ROWS, WIDTH:], tail], axis=1)
    for copy in sends:
        copy.wait_send()
    row_out.wait_send()
    for i in range(NZ):

        @pl.when(jnp.logical_and(z >= i, z < NZ - 1))
        def _():
            az_up(i).wait_send()

        if i > 0:

            @pl.when(z >= i)
            def _():
                az_down(i).wait_send()

        @pl.when(z != i)
        def _():
            rz(i).wait_send()

    hid_copy.wait()


def on_device(tokens, hidden_grad, master, counts):
    rows, depth = tokens.shape
    chunk = depth // NZ
    dma = pltpu.SemaphoreType.DMA
    vmem = pltpu.VMEM
    hidden, weight_grad = pl.pallas_call(
        kernel,
        out_shape=(
            jax.ShapeDtypeStruct((WIDTH, rows), BF16),
            jax.ShapeDtypeStruct(master.shape, F32),
        ),
        in_specs=[
            pl.BlockSpec(memory_space=pl.ANY),
            pl.BlockSpec(memory_space=pl.ANY),
            pl.BlockSpec(memory_space=vmem),
            pl.BlockSpec(memory_space=pltpu.SMEM),
        ],
        out_specs=(pl.BlockSpec(memory_space=pl.ANY), pl.BlockSpec(memory_space=vmem)),
        scratch_shapes=[
            vmem((NZ, rows, chunk), BF16),
            vmem((NZ, NY, chunk // NY, rows), BF16),
            vmem((WIDTH, rows), BF16),
            vmem((2, NY, NZ, PACKED, 128), BF16),
            vmem((chunk, 2 * WIDTH), BF16),
            vmem((2 * WIDTH, rows), F32),
            vmem((2 * WIDTH, rows), BF16),
            vmem((WIDTH, rows), BF16),
            vmem((8, 8, 128), jnp.int32),
            vmem((NY, NZ, 2, ROWS, 2 * WIDTH), F32),
            vmem((NY, NZ, PACKED, 128), BF16),
            vmem((NY, NZ, PACKED, 128), BF16),
            vmem((2, 4, NZ, PACKED, 128), BF16),
            vmem((2, 4, NZ, PACKED, 128), BF16),
            vmem((NY, NZ, PACKED, 128), F32),
            vmem((NZ, PACKED, 128), BF16),
            vmem((NZ, PACKED, 128), BF16),
            dma((NZ,)), dma, dma,
            dma((3,)), dma((3,)), dma, dma, dma((NZ,)), dma((NZ,)), dma((NZ,)),
            dma((2, 4, 4)), dma((2, 4, 4)), dma((NY, 4)), dma((NY, 4)),
            dma((NY,)), dma((NY,)), dma((2, 4, 4)), dma((2, 4, 4)), dma((NZ,)), dma((NZ,)),
        ],
        compiler_params=pltpu.CompilerParams(
            collective_id=1, has_side_effects=True, vmem_limit_bytes=56 * 2**20
        ),
    )(tokens, hidden_grad.T, master, counts)
    return hidden.T, weight_grad


def solution(mesh):
    return jax.shard_map(
        on_device,
        mesh=mesh,
        in_specs=(
            P("node", None),
            P("node", "local"),
            P(None, "node", "local"),
            P(("node", "local")),
        ),
        out_specs=(P("node", "local"), P(None, "node", "local")),
        check_vma=False,
    )
```

```python
import jax
import jax.numpy as jnp
from jax import lax
from jax.experimental import pallas as pl
from jax.experimental.pallas import tpu as pltpu
from jax.sharding import PartitionSpec as P

BF16 = jnp.bfloat16
F32 = jnp.float32
MESH = pl.DeviceIdType.MESH

NZ, NY = 8, 8
ROWS, WIDTH = 32, 96
PACKED = 48


def pack(block):
    tail = jnp.concatenate([block[..., :16, 128:192], block[..., 16:32, 128:192]], axis=-1)
    return jnp.concatenate([block[..., :128], tail], axis=-2)


def kernel(
    tok_hbm, hgT_hbm, master_hbm, counts_hbm,
    hidT_hbm, wg_ref,
    master_ref, counts_ref, tok, tokT, hgT, wbuf, w_y, acc, cotT, hidT, cnt,
    part, xsend, xrecv, rsend, rrecv, own, zsend, zrecv,
    tok_sem, hg_sem, hid_sem, small_sem,
    cx_s, cx_r, ch_s, ch_r, az_u, az_d, az_r, ay_s, ay_r, ac_s, ac_r,
    rc_s, rc_r, ry_s, ry_r, rz_s, rz_r,
):
    node, loc = lax.axis_index("node"), lax.axis_index("local")
    z, y, c = node // (2 * NY), (node // 2) % NY, node % 2
    zh, x = loc // 4, loc % 4
    rows = tok.shape[1]
    chunk = tok.shape[2]

    def at(z_, y_, c_):
        return ((z_ * NY + y_) * 2 + c_, loc)

    def ring(offset):
        return lax.rem(y + offset + 2 * NY, NY)

    right, left, twin = at(z, ring(1), c), at(z, ring(-1), c), at(z, y, 1 - c)
    x_peers = [(node, zh * 4 + lax.rem(x + i, 4)) for i in range(1, 4)]
    partner = (node, (1 - zh) * 4 + x)

    tok_copies = [
        pltpu.make_async_copy(tok_hbm.at[:, pl.ds(i * chunk, chunk)], tok.at[i], tok_sem.at[i])
        for i in range(NZ)
    ]
    hg_copy = pltpu.make_async_copy(hgT_hbm, hgT, hg_sem)
    hid_copy = pltpu.make_async_copy(hidT, hidT_hbm, hid_sem)

    small = [
        pltpu.make_async_copy(master_hbm, master_ref, small_sem.at[0]),
        pltpu.make_async_copy(counts_hbm, counts_ref, small_sem.at[1]),
    ]
    for copy in small:
        copy.start()

    gate_z = NZ // 2 - 1
    low = z % 4
    barrier = pltpu.get_barrier_semaphore()

    def greet(peer):
        pl.semaphore_signal(barrier, inc=1, device_id=peer, device_id_type=MESH)

    for i in range(1, NZ):

        @pl.when(z + i < NZ)
        def _():
            greet(at(z + i, y, c))

    for i in range(1, 4):

        @pl.when(low >= i)
        def _():
            greet(at(z - i, y, c))

    @pl.when(z > gate_z)
    def _():
        greet(at(gate_z, y, c))

    @pl.when(zh == 0)
    def _():
        greet(partner)

    for peer in [right, left, twin] + x_peers:
        greet(peer)
    for copy in small:
        copy.wait()
    both = jnp.concatenate([master_ref[0], master_ref[1]], axis=1)
    wbuf[c, y, z] = pack(both).astype(BF16)
    cnt[loc] = jnp.full((8, 128), counts_ref[0], jnp.int32)
    pl.semaphore_wait(barrier, 9 - low + z + zh + jnp.where(z == gate_z, 4, 0))

    sends = []

    def remote(src, dst, s_sem, r_sem, device):
        return pltpu.make_async_remote_copy(
            src_ref=src, dst_ref=dst, send_sem=s_sem, recv_sem=r_sem,
            device_id=device, device_id_type=MESH,
        )

    def push(copy):
        copy.start()
        sends.append(copy)

    def transpose(i):
        tok_copies[i].wait()
        tokT[i] = tok[i].T.reshape(NY, chunk // NY, rows)

    pz, ph = z // 2, z // 4
    pairs = [pz, ph * 4 + 1 - pz, 2 - ph, 3 - 3 * ph]

    def pair(k):
        return pl.ds(2 * pairs[k], 2)

    def az_down(i):
        block = wbuf.at[c, y, z]
        return remote(block, block, az_d.at[i], az_r.at[z], at(z - i, y, c))

    def az_up(f, i):
        block = wbuf.at[c, y, z - f]
        return remote(block, block, az_u.at[f, i], az_r.at[z - f], at(z + i, y, c))

    def az_wait(origin):
        block = wbuf.at[c, y, origin]
        remote(block, block, az_d.at[0], az_r.at[origin], twin).wait_recv()

    def up_has(i):
        return jnp.logical_or(low + i < 4, z == gate_z)

    def pass_up(f):
        @pl.when(z == gate_z)
        def _():
            az_wait(z - f)
            for i in range(4, 0, -1):
                az_up(f, i).start()

    for i in range(4, 0, -1):

        @pl.when(up_has(i))
        def _():
            az_up(0, i).start()

    for i in range(NZ - 1, 0, -1):

        @pl.when(z >= i)
        def _():
            az_down(i).start()

    for i in range(3):
        push(remote(cnt.at[loc], cnt.at[loc], cx_s.at[i], cx_r.at[2 - i], x_peers[i]))
    for copy in tok_copies:
        copy.start()
    hg_copy.start()

    def ay(d, s, k):
        origin = ring(1 - s) if d == 0 else ring(s - 1)
        block = wbuf.at[c, origin, pair(k)]
        return remote(block, block, ay_s.at[d, s - 1, k], ay_r.at[d, s - 1, k], right if d == 0 else left)

    def ac(offset, k, core):
        block = wbuf.at[core, ring(offset), pair(k)]
        return remote(block, block, ac_s.at[offset % NY, k], ac_r.at[offset % NY, k], twin)

    def forward(offset):
        for k in range(4):
            ac(offset, k, 1 - c).wait_recv()
        o = ring(offset)
        for core in range(2):
            for j in range(NZ):
                r = j * 64 + core * ROWS
                got = wbuf[core, o, j]
                w_y[r : r + ROWS, :128] = got[:ROWS]
                w_y[r : r + 16, 128:192] = got[ROWS:, :64]
                w_y[r + 16 : r + 32, 128:192] = got[ROWS:, 64:]
        v = tokT[:, o].reshape(chunk, rows)
        d = lax.dot_general(w_y[...], v, (((0,), (0,)), ((), ())), preferred_element_type=F32)
        if offset == 0:
            acc[...] = d
        else:
            acc[...] += d

    def gather(k, s):
        if s == 0:
            for i in range(2):
                origin = 2 * pairs[k] + i

                @pl.when(jnp.logical_and(origin != z, jnp.logical_or(z != gate_z, origin > z)))
                def _():
                    az_wait(origin)

            for d in range(2):
                push(ay(d, 1, k))
            push(ac(0, k, c))
            return
        for d in range(2):
            if s == 4 and d != k % 2:
                continue
            ay(d, s, k).wait_recv()
            if s < 3 or (s == 3 and d == k % 2):
                push(ay(d, s + 1, k))
            push(ac(4 if s == 4 else (-s if d == 0 else s), k, c))

    own_row = cnt.at[pl.ds(zh * 4, 4)]
    other_row = cnt.at[pl.ds((1 - zh) * 4, 4)]
    row_out = remote(own_row, own_row, ch_s, ch_r, partner)
    row_in = remote(other_row, other_row, ch_s, ch_r, partner)

    for t in range(8):
        if t == 0:
            pass_up(1)
        elif t == 1:
            pass_up(3)
        elif t < 4:
            pass
        elif t == 4:
            forward(0)
        else:
            forward(t - 4)
            forward(4 - t)
        for k in range(4):
            if 0 <= t - k <= 4:
                gather(k, t - k)
        if t == 0:
            pass_up(2)
        for i in ([0], [1, 2], [3, 4], [5, 6, 7], [], [], [], [])[t]:
            transpose(i)
        if t == 1:
            for i in range(3):
                slot = cnt.at[zh * 4 + lax.rem(x + 3 - i, 4)]
                remote(slot, slot, cx_s.at[i], cx_r.at[2 - i], twin).wait_recv()

            @pl.when(zh == 1)
            def _():
                row_out.start()

    row_in.wait_recv()

    @pl.when(zh == 0)
    def _():
        row_out.start()

    forward(4)

    for j in range(8):
        lanes = slice(j * 128, (j + 1) * 128)
        live = (lax.broadcasted_iota(jnp.int32, (8, 128), 1) < cnt[j]).astype(F32)[:1]
        gate, up = acc[:WIDTH, lanes], acc[WIDTH:, lanes]
        if j == 0:
            hg_copy.wait()
        sig = jax.nn.sigmoid(gate)
        activated = gate * sig
        hidT[:, lanes] = (live * activated * up).astype(BF16)
        upstream = live * hgT[:, lanes].astype(F32)
        cotT[:WIDTH, lanes] = (upstream * up * sig * (1.0 + gate * (1.0 - sig))).astype(BF16)
        cotT[WIDTH:, lanes] = (upstream * activated).astype(BF16)
    hid_copy.start()

    def rc(offset):
        i = offset % NY
        return remote(xsend.at[i], xrecv.at[i], rc_s.at[i], rc_r.at[i], twin)

    def backward(offset):
        i = offset % NY
        v = tokT[:, ring(offset)].reshape(chunk, rows)
        g = lax.dot_general(v, cotT[...], (((1,), (1,)), ((), ())), preferred_element_type=F32)
        part[i] = g.reshape(NZ, 2, ROWS, 2 * WIDTH)
        xsend[i] = pack(part[i, :, 1 - c]).astype(BF16)
        push(rc(offset))

    def chip_sum(offset):
        i = offset % NY
        rc(offset).wait_recv()
        own[i] = pack(part[i, :, c]) + xrecv[i].astype(F32)

    def ry(d, s, k):
        return remote(
            rsend.at[d, s - 1, pair(k)], rrecv.at[d, s - 1, pair(k)],
            ry_s.at[d, s - 1, k], ry_r.at[d, s - 1, k], right if d == 0 else left,
        )

    def ry_send(s):
        for k in range(3, -1, -1):
            for d in range(2):
                if s == 1 and d != k % 2:
                    continue
                mine = own[(5 - s if d == 0 else s - 5) % NY, pair(k)]
                if s > 2 or (s == 2 and d == k % 2):
                    ry(d, s - 1, k).wait_recv()
                    mine = mine + rrecv[d, s - 2, pair(k)].astype(F32)
                rsend[d, s - 1, pair(k)] = mine.astype(BF16)
                push(ry(d, s, k))

    backward(4)
    backward(3)
    chip_sum(4)
    ry_send(1)
    backward(-3)
    chip_sum(3)
    backward(2)
    chip_sum(-3)
    ry_send(2)
    backward(-2)
    chip_sum(2)
    backward(1)
    chip_sum(-2)
    ry_send(3)
    backward(-1)
    chip_sum(1)
    backward(0)
    chip_sum(-1)
    ry_send(4)
    chip_sum(0)
    zrecv[z] = jnp.zeros(zrecv.shape[1:], BF16)

    def rz(to):
        return remote(zsend.at[to], zrecv.at[z], rz_s.at[to], rz_r.at[z], at(to, y, c))

    for k in range(3, -1, -1):
        total = own[0, pair(k)]
        for d in range(2):
            ry(d, 4, k).wait_recv()
            total = total + rrecv[d, 3, pair(k)].astype(F32)
        own[0, pair(k)] = total
        zsend[pair(k)] = total.astype(BF16)
        for i in range(2):
            to = 2 * pairs[k] + i

            @pl.when(to != z)
            def _():
                rz(to).start()

    for j in range(NZ):

        @pl.when(z != j)
        def _():
            remote(zsend.at[j], zrecv.at[j], rz_s.at[j], rz_r.at[j], twin).wait_recv()

    grad = own[0, z]
    for j in range(NZ):
        grad = grad + zrecv[j].astype(F32)
    grad = grad * (1.0 / (rows * NZ * NY * 2) ** 0.5)
    tail = jnp.concatenate([grad[ROWS:, :64], grad[ROWS:, 64:]], axis=0)
    wg_ref[0] = grad[:ROWS, :WIDTH]
    wg_ref[1] = jnp.concatenate([grad[:ROWS, WIDTH:], tail], axis=1)
    for copy in sends:
        copy.wait_send()
    row_out.wait_send()
    for i in range(1, 5):

        @pl.when(up_has(i))
        def _():
            az_up(0, i).wait_send()

        @pl.when(z == gate_z)
        def _():
            for f in range(1, 4):
                az_up(f, i).wait_send()

    for i in range(NZ):
        if i > 0:

            @pl.when(z >= i)
            def _():
                az_down(i).wait_send()

        @pl.when(z != i)
        def _():
            rz(i).wait_send()

    hid_copy.wait()


def hand_out(hidden_in, grad_in, hidden_out, grad_out):
    hidden_out[...] = hidden_in[...]
    grad_out[...] = grad_in[...]


def on_device(tokens, hidden_grad, master, counts):
    rows, depth = tokens.shape
    chunk = depth // NZ
    dma = pltpu.SemaphoreType.DMA
    vmem = pltpu.VMEM
    hidden, weight_grad = pl.pallas_call(
        kernel,
        out_shape=(
            jax.ShapeDtypeStruct((WIDTH, rows), BF16),
            jax.ShapeDtypeStruct(master.shape, F32),
        ),
        in_specs=[
            pl.BlockSpec(memory_space=pl.ANY),
            pl.BlockSpec(memory_space=pl.ANY),
            pl.BlockSpec(memory_space=pltpu.HBM),
            pl.BlockSpec(memory_space=pltpu.HBM),
        ],
        out_specs=(pl.BlockSpec(memory_space=pl.ANY), pl.BlockSpec(memory_space=vmem)),
        scratch_shapes=[
            vmem(master.shape, F32),
            pltpu.SMEM(counts.shape, jnp.int32),
            vmem((NZ, rows, chunk), BF16),
            vmem((NZ, NY, chunk // NY, rows), BF16),
            vmem((WIDTH, rows), BF16),
            vmem((2, NY, NZ, PACKED, 128), BF16),
            vmem((chunk, 2 * WIDTH), BF16),
            vmem((2 * WIDTH, rows), F32),
            vmem((2 * WIDTH, rows), BF16),
            vmem((WIDTH, rows), BF16),
            vmem((8, 8, 128), jnp.int32),
            vmem((NY, NZ, 2, ROWS, 2 * WIDTH), F32),
            vmem((NY, NZ, PACKED, 128), BF16),
            vmem((NY, NZ, PACKED, 128), BF16),
            vmem((2, 4, NZ, PACKED, 128), BF16),
            vmem((2, 4, NZ, PACKED, 128), BF16),
            vmem((NY, NZ, PACKED, 128), F32),
            vmem((NZ, PACKED, 128), BF16),
            vmem((NZ, PACKED, 128), BF16),
            dma((NZ,)), dma, dma, dma((2,)),
            dma((3,)), dma((3,)), dma, dma, dma((4, 5)), dma((NZ,)), dma((NZ,)),
            dma((2, 4, 4)), dma((2, 4, 4)), dma((NY, 4)), dma((NY, 4)),
            dma((NY,)), dma((NY,)), dma((2, 4, 4)), dma((2, 4, 4)), dma((NZ,)), dma((NZ,)),
        ],
        compiler_params=pltpu.CompilerParams(
            collective_id=1, has_side_effects=True, vmem_limit_bytes=56 * 2**20
        ),
    )(tokens, hidden_grad.T, master, counts)
    hidden, weight_grad = pl.pallas_call(
        hand_out,
        out_shape=(
            jax.ShapeDtypeStruct(hidden.shape, BF16),
            jax.ShapeDtypeStruct(master.shape, F32),
        ),
        in_specs=[pl.BlockSpec(memory_space=vmem)] * 2,
        out_specs=(pl.BlockSpec(memory_space=vmem),) * 2,
    )(hidden, weight_grad)
    return hidden.T, weight_grad


def solution(mesh):
    return jax.shard_map(
        on_device,
        mesh=mesh,
        in_specs=(
            P("node", None),
            P("node", "local"),
            P(None, "node", "local"),
            P(("node", "local")),
        ),
        out_specs=(P("node", "local"), P(None, "node", "local")),
        check_vma=False,
    )
```

```python
import jax
import jax.numpy as jnp
from jax import lax
from jax.experimental import pallas as pl
from jax.experimental.pallas import tpu as pltpu
from jax.sharding import PartitionSpec as P

BF16 = jnp.bfloat16
F32 = jnp.float32
MESH = pl.DeviceIdType.MESH

NZ, NY = 8, 8
ROWS, WIDTH = 32, 96
PACKED = 48
FAR_OUT = (3,)
FAR_IN = (3,)


def pack(block):
    tail = jnp.concatenate([block[..., :16, 128:192], block[..., 16:32, 128:192]], axis=-1)
    return jnp.concatenate([block[..., :128], tail], axis=-2)


def kernel(
    tok_hbm, hgT_hbm, master_hbm, counts_hbm,
    hidT_hbm, wg_ref,
    master_ref, counts_ref, tok, tokT, hgT, wbuf, w_y, acc, cotT, hidT, cnt,
    part, xsend, xrecv, rsend, rrecv, dsend, drecv, own, zsend, zrecv,
    tok_sem, hg_sem, hid_sem, small_sem,
    cx_s, cx_r, ch_s, ch_r, az_u, az_d, az_r, ay_s, ay_r, ac_s, ac_r,
    rc_s, rc_r, ry_s, ry_r, rz_s, rz_r, ad_s, ad_r, rd_s, rd_r,
):
    node, loc = lax.axis_index("node"), lax.axis_index("local")
    z, y, c = node // (2 * NY), (node // 2) % NY, node % 2
    zh, x = loc // 4, loc % 4
    rows = tok.shape[1]
    chunk = tok.shape[2]

    def at(z_, y_, c_):
        return ((z_ * NY + y_) * 2 + c_, loc)

    def ring(offset):
        return lax.rem(y + offset + 2 * NY, NY)

    right, left, twin = at(z, ring(1), c), at(z, ring(-1), c), at(z, y, 1 - c)
    x_peers = [(node, zh * 4 + lax.rem(x + i, 4)) for i in range(1, 4)]
    partner = (node, (1 - zh) * 4 + x)

    tok_copies = [
        pltpu.make_async_copy(tok_hbm.at[:, pl.ds(i * chunk, chunk)], tok.at[i], tok_sem.at[i])
        for i in range(NZ)
    ]
    hg_copy = pltpu.make_async_copy(hgT_hbm, hgT, hg_sem)
    hid_copy = pltpu.make_async_copy(hidT, hidT_hbm, hid_sem)

    small = [
        pltpu.make_async_copy(master_hbm, master_ref, small_sem.at[0]),
        pltpu.make_async_copy(counts_hbm, counts_ref, small_sem.at[1]),
    ]
    for copy in small:
        copy.start()

    gate_z = NZ // 2 - 1
    low = z % 4
    barrier = pltpu.get_barrier_semaphore()

    def greet(peer):
        pl.semaphore_signal(barrier, inc=1, device_id=peer, device_id_type=MESH)

    for i in range(1, NZ):

        @pl.when(z + i < NZ)
        def _():
            greet(at(z + i, y, c))

    for i in range(1, 4):

        @pl.when(low >= i)
        def _():
            greet(at(z - i, y, c))

    @pl.when(z > gate_z)
    def _():
        greet(at(gate_z, y, c))

    @pl.when(zh == 0)
    def _():
        greet(partner)

    for peer in [right, left, twin] + x_peers:
        greet(peer)
    for copy in small:
        copy.wait()
    both = jnp.concatenate([master_ref[0], master_ref[1]], axis=1)
    wbuf[c, y, z] = pack(both).astype(BF16)
    cnt[loc] = jnp.full((8, 128), counts_ref[0], jnp.int32)
    pl.semaphore_wait(barrier, 9 - low + z + zh + jnp.where(z == gate_z, 4, 0))

    sends = []

    def remote(src, dst, s_sem, r_sem, device):
        return pltpu.make_async_remote_copy(
            src_ref=src, dst_ref=dst, send_sem=s_sem, recv_sem=r_sem,
            device_id=device, device_id_type=MESH,
        )

    def push(copy):
        copy.start()
        sends.append(copy)

    def transpose(i):
        tok_copies[i].wait()
        tokT[i] = tok[i].T.reshape(NY, chunk // NY, rows)

    pz, ph = z // 2, z // 4
    pairs = [pz, ph * 4 + 1 - pz, 2 - ph, 3 - 3 * ph]

    def pair(k):
        return pl.ds(2 * pairs[k], 2)

    def az_down(i):
        block = wbuf.at[c, y, z]
        return remote(block, block, az_d.at[i], az_r.at[z], at(z - i, y, c))

    def az_up(f, i):
        block = wbuf.at[c, y, z - f]
        return remote(block, block, az_u.at[f, i], az_r.at[z - f], at(z + i, y, c))

    def az_wait(origin):
        block = wbuf.at[c, y, origin]
        remote(block, block, az_d.at[0], az_r.at[origin], twin).wait_recv()

    def up_has(i):
        return jnp.logical_or(low + i < 4, z == gate_z)

    def pass_up(f):
        @pl.when(z == gate_z)
        def _():
            az_wait(z - f)
            for i in range(4, 0, -1):
                az_up(f, i).start()

    for i in range(4, 0, -1):

        @pl.when(up_has(i))
        def _():
            az_up(0, i).start()

    for i in range(NZ - 1, 0, -1):

        @pl.when(z >= i)
        def _():
            az_down(i).start()

    for i in range(3):
        push(remote(cnt.at[loc], cnt.at[loc], cx_s.at[i], cx_r.at[2 - i], x_peers[i]))
    for copy in tok_copies:
        copy.start()
    hg_copy.start()

    def ay(d, s, k):
        origin = ring(1 - s) if d == 0 else ring(s - 1)
        block = wbuf.at[c, origin, pair(k)]
        return remote(block, block, ay_s.at[d, s - 1, k], ay_r.at[d, s - 1, k], right if d == 0 else left)

    def ac(offset, k, core):
        block = wbuf.at[core, ring(offset), pair(k)]
        return remote(block, block, ac_s.at[offset % NY, k], ac_r.at[offset % NY, k], twin)

    def forward(offset):
        for k in range(4):
            ac(offset, k, 1 - c).wait_recv()
        o = ring(offset)
        for core in range(2):
            for j in range(NZ):
                r = j * 64 + core * ROWS
                got = wbuf[core, o, j]
                w_y[r : r + ROWS, :128] = got[:ROWS]
                w_y[r : r + 16, 128:192] = got[ROWS:, :64]
                w_y[r + 16 : r + 32, 128:192] = got[ROWS:, 64:]
        v = tokT[:, o].reshape(chunk, rows)
        d = lax.dot_general(w_y[...], v, (((0,), (0,)), ((), ())), preferred_element_type=F32)
        if offset == 0:
            acc[...] = d
        else:
            acc[...] += d

    def ad(offset, k):
        block = wbuf.at[c, y, pair(k)]
        i = offset % NY
        return remote(block, block, ad_s.at[i, k], ad_r.at[i, k], at(z, ring(offset), c))

    def gather(k, s):
        if s == 0:
            for i in range(2):
                origin = 2 * pairs[k] + i

                @pl.when(jnp.logical_and(origin != z, jnp.logical_or(z != gate_z, origin > z)))
                def _():
                    az_wait(origin)

            if k in FAR_OUT:
                for offset in (3, -3, 2, -2, 1, -1):
                    push(ad(offset, k))
            else:
                for d in range(2):
                    push(ay(d, 1, k))
            push(ac(0, k, c))
            return
        if k in FAR_OUT:
            for offset in (4,) if s == 4 else (s, -s):
                ad(offset, k).wait_recv()
                push(ac(-offset if s < 4 else 4, k, c))
            return
        for d in range(2):
            if s == 4 and d != k % 2:
                continue
            ay(d, s, k).wait_recv()
            if s < 3 or (s == 3 and d == k % 2):
                push(ay(d, s + 1, k))
            push(ac(4 if s == 4 else (-s if d == 0 else s), k, c))

    own_row = cnt.at[pl.ds(zh * 4, 4)]
    other_row = cnt.at[pl.ds((1 - zh) * 4, 4)]
    row_out = remote(own_row, own_row, ch_s, ch_r, partner)
    row_in = remote(other_row, other_row, ch_s, ch_r, partner)

    for t in range(8):
        if t == 0:
            pass_up(1)
        elif t == 1:
            pass_up(3)
        elif t < 4:
            pass
        elif t == 4:
            forward(0)
        else:
            forward(t - 4)
            forward(4 - t)
        for k in range(4):
            if 0 <= t - k <= 4:
                gather(k, t - k)
            if t == 4 and k == 0:
                for far in FAR_OUT:
                    push(ad(4, far))
        if t == 0:
            pass_up(2)
        for i in ([0], [1, 2], [3, 4], [5, 6, 7], [], [], [], [])[t]:
            transpose(i)
        if t == 1:
            for i in range(3):
                slot = cnt.at[zh * 4 + lax.rem(x + 3 - i, 4)]
                remote(slot, slot, cx_s.at[i], cx_r.at[2 - i], twin).wait_recv()

            @pl.when(zh == 1)
            def _():
                row_out.start()

    row_in.wait_recv()

    @pl.when(zh == 0)
    def _():
        row_out.start()

    forward(4)

    for j in range(8):
        lanes = slice(j * 128, (j + 1) * 128)
        live = (lax.broadcasted_iota(jnp.int32, (8, 128), 1) < cnt[j]).astype(F32)[:1]
        gate, up = acc[:WIDTH, lanes], acc[WIDTH:, lanes]
        if j == 0:
            hg_copy.wait()
        sig = jax.nn.sigmoid(gate)
        activated = gate * sig
        hidT[:, lanes] = (live * activated * up).astype(BF16)
        upstream = live * hgT[:, lanes].astype(F32)
        cotT[:WIDTH, lanes] = (upstream * up * sig * (1.0 + gate * (1.0 - sig))).astype(BF16)
        cotT[WIDTH:, lanes] = (upstream * activated).astype(BF16)
    hid_copy.start()

    def rc(offset):
        i = offset % NY
        return remote(xsend.at[i], xrecv.at[i], rc_s.at[i], rc_r.at[i], twin)

    def backward(offset):
        i = offset % NY
        v = tokT[:, ring(offset)].reshape(chunk, rows)
        g = lax.dot_general(v, cotT[...], (((1,), (1,)), ((), ())), preferred_element_type=F32)
        part[i] = g.reshape(NZ, 2, ROWS, 2 * WIDTH)
        xsend[i] = pack(part[i, :, 1 - c]).astype(BF16)
        push(rc(offset))

    def chip_sum(offset):
        i = offset % NY
        rc(offset).wait_recv()
        own[i] = pack(part[i, :, c]) + xrecv[i].astype(F32)
        if i:
            for k in FAR_IN:
                dsend[i, pair(k)] = own[i, pair(k)].astype(BF16)
                push(rd(offset, k))

    def rd(offset, k):
        i = offset % NY
        return remote(
            dsend.at[i, pair(k)], drecv.at[i, pair(k)], rd_s.at[i, k], rd_r.at[i, k], at(z, ring(offset), c)
        )

    def ry(d, s, k):
        return remote(
            rsend.at[d, s - 1, pair(k)], rrecv.at[d, s - 1, pair(k)],
            ry_s.at[d, s - 1, k], ry_r.at[d, s - 1, k], right if d == 0 else left,
        )

    def ry_send(s):
        for k in range(3, -1, -1):
            if k in FAR_IN:
                continue
            for d in range(2):
                if s == 1 and d != k % 2:
                    continue
                mine = own[(5 - s if d == 0 else s - 5) % NY, pair(k)]
                if s > 2 or (s == 2 and d == k % 2):
                    ry(d, s - 1, k).wait_recv()
                    mine = mine + rrecv[d, s - 2, pair(k)].astype(F32)
                rsend[d, s - 1, pair(k)] = mine.astype(BF16)
                push(ry(d, s, k))

    backward(4)
    backward(3)
    chip_sum(4)
    ry_send(1)
    backward(-3)
    chip_sum(3)
    backward(2)
    chip_sum(-3)
    ry_send(2)
    backward(-2)
    chip_sum(2)
    backward(1)
    chip_sum(-2)
    ry_send(3)
    backward(-1)
    chip_sum(1)
    backward(0)
    chip_sum(-1)
    ry_send(4)
    chip_sum(0)
    zrecv[z] = jnp.zeros(zrecv.shape[1:], BF16)

    def rz(to):
        return remote(zsend.at[to], zrecv.at[z], rz_s.at[to], rz_r.at[z], at(to, y, c))

    for k in range(3, -1, -1):
        total = own[0, pair(k)]
        if k in FAR_IN:
            for offset in (4, 3, -3, 2, -2, 1, -1):
                rd(offset, k).wait_recv()
                total = total + drecv[offset % NY, pair(k)].astype(F32)
        else:
            for d in range(2):
                ry(d, 4, k).wait_recv()
                total = total + rrecv[d, 3, pair(k)].astype(F32)
        own[0, pair(k)] = total
        zsend[pair(k)] = total.astype(BF16)
        for i in range(2):
            to = 2 * pairs[k] + i

            @pl.when(to != z)
            def _():
                rz(to).start()

    for j in range(NZ):

        @pl.when(z != j)
        def _():
            remote(zsend.at[j], zrecv.at[j], rz_s.at[j], rz_r.at[j], twin).wait_recv()

    grad = own[0, z]
    for j in range(NZ):
        grad = grad + zrecv[j].astype(F32)
    grad = grad * (1.0 / (rows * NZ * NY * 2) ** 0.5)
    tail = jnp.concatenate([grad[ROWS:, :64], grad[ROWS:, 64:]], axis=0)
    wg_ref[0] = grad[:ROWS, :WIDTH]
    wg_ref[1] = jnp.concatenate([grad[:ROWS, WIDTH:], tail], axis=1)
    for copy in sends:
        copy.wait_send()
    row_out.wait_send()
    for i in range(1, 5):

        @pl.when(up_has(i))
        def _():
            az_up(0, i).wait_send()

        @pl.when(z == gate_z)
        def _():
            for f in range(1, 4):
                az_up(f, i).wait_send()

    for i in range(NZ):
        if i > 0:

            @pl.when(z >= i)
            def _():
                az_down(i).wait_send()

        @pl.when(z != i)
        def _():
            rz(i).wait_send()

    hid_copy.wait()


def hand_out(hidden_in, grad_in, hidden_out, grad_out):
    hidden_out[...] = hidden_in[...]
    grad_out[...] = grad_in[...]


def on_device(tokens, hidden_grad, master, counts):
    rows, depth = tokens.shape
    chunk = depth // NZ
    dma = pltpu.SemaphoreType.DMA
    vmem = pltpu.VMEM
    hidden, weight_grad = pl.pallas_call(
        kernel,
        out_shape=(
            jax.ShapeDtypeStruct((WIDTH, rows), BF16),
            jax.ShapeDtypeStruct(master.shape, F32),
        ),
        in_specs=[
            pl.BlockSpec(memory_space=pl.ANY),
            pl.BlockSpec(memory_space=pl.ANY),
            pl.BlockSpec(memory_space=pltpu.HBM),
            pl.BlockSpec(memory_space=pltpu.HBM),
        ],
        out_specs=(pl.BlockSpec(memory_space=pl.ANY), pl.BlockSpec(memory_space=vmem)),
        scratch_shapes=[
            vmem(master.shape, F32),
            pltpu.SMEM(counts.shape, jnp.int32),
            vmem((NZ, rows, chunk), BF16),
            vmem((NZ, NY, chunk // NY, rows), BF16),
            vmem((WIDTH, rows), BF16),
            vmem((2, NY, NZ, PACKED, 128), BF16),
            vmem((chunk, 2 * WIDTH), BF16),
            vmem((2 * WIDTH, rows), F32),
            vmem((2 * WIDTH, rows), BF16),
            vmem((WIDTH, rows), BF16),
            vmem((8, 8, 128), jnp.int32),
            vmem((NY, NZ, 2, ROWS, 2 * WIDTH), F32),
            vmem((NY, NZ, PACKED, 128), BF16),
            vmem((NY, NZ, PACKED, 128), BF16),
            vmem((2, 4, NZ, PACKED, 128), BF16),
            vmem((2, 4, NZ, PACKED, 128), BF16),
            vmem((NY, NZ, PACKED, 128), BF16),
            vmem((NY, NZ, PACKED, 128), BF16),
            vmem((NY, NZ, PACKED, 128), F32),
            vmem((NZ, PACKED, 128), BF16),
            vmem((NZ, PACKED, 128), BF16),
            dma((NZ,)), dma, dma, dma((2,)),
            dma((3,)), dma((3,)), dma, dma, dma((4, 5)), dma((NZ,)), dma((NZ,)),
            dma((2, 4, 4)), dma((2, 4, 4)), dma((NY, 4)), dma((NY, 4)),
            dma((NY,)), dma((NY,)), dma((2, 4, 4)), dma((2, 4, 4)), dma((NZ,)), dma((NZ,)),
            dma((NY, 4)), dma((NY, 4)), dma((NY, 4)), dma((NY, 4)),
        ],
        compiler_params=pltpu.CompilerParams(
            collective_id=1, has_side_effects=True, vmem_limit_bytes=56 * 2**20
        ),
    )(tokens, hidden_grad.T, master, counts)
    hidden, weight_grad = pl.pallas_call(
        hand_out,
        out_shape=(
            jax.ShapeDtypeStruct(hidden.shape, BF16),
            jax.ShapeDtypeStruct(master.shape, F32),
        ),
        in_specs=[pl.BlockSpec(memory_space=vmem)] * 2,
        out_specs=(pl.BlockSpec(memory_space=vmem),) * 2,
    )(hidden, weight_grad)
    return hidden.T, weight_grad


def solution(mesh):
    return jax.shard_map(
        on_device,
        mesh=mesh,
        in_specs=(
            P("node", None),
            P("node", "local"),
            P(None, "node", "local"),
            P(("node", "local")),
        ),
        out_specs=(P("node", "local"), P(None, "node", "local")),
        check_vma=False,
    )
```
